512 devices in a mesh: rows: 32 (over x, y), cols: 16 (over z, core).
Axes of the slice: x: 4, y: 8, z: 8, core: 2. Of those that a mesh axis runs over, the one named last changes fastest.
Arguments:
- tiles: bfloat16 [32, 16, 16, 128, 8, 128], P('rows', 'cols'), may hold values from -64 to 64, as said below
- tile_coords: int32 [32, 16, 16, 2], P('rows', 'cols'), may hold values from 0 to 63, as said below
- tile_counts: int32 [32, 16, 1], P('rows', 'cols'), may hold values from 8 to 16, as said below
- factor_two: bfloat16 [131072, 256], P(('cols', 'rows')), may hold values from -6 to 6
- factor_three: bfloat16 [8, 256], replicated, may hold values from -6 to 6
- sketch_two: bfloat16 [256, 256], replicated, may hold values from -0.375 to 0.375
- sketch_three: bfloat16 [256, 256], replicated, may hold values from -0.375 to 0.375
Outputs:
- new_factor: float32 [65536, 256], P(('rows', 'cols'))
The draws below stay inside these ranges and needn't reach their ends.
Inputs may be any that keep to these rules, and one draw needn't show every extreme that they name: `tile_coords`: column 0 is a mode-1 block within the row group, below 16; column 1 a mode-2 block within the column group, below 64. Slot 0 of device (r, c) is live and has mode-1 block c and mode-2 block r * 2 + 1, so every mode-1 block has a tile. Dead slots hold valid coordinates too. `tile_counts`: every device with column index 0 is full. `tiles`: dead slots hold arbitrary values.
All inputs are finite; a program needn't handle non-finite values.
Results may differ from the reference program's by a relative error of at most 0.0041.
Values may be sent and summed in bfloat16 or wider, within the bound.
A program may use at most 64 MiB of HBM per device.

```python
import jax
import jax.numpy as jnp
from jax import lax

BLK = 128
RANK = 256
KS = 8
CAP = 16
JBD = 2
NI = 65536
NJ = 131072
N_ROWS = 32
N_COLS = 16


def draw_tiles(key, part):
    key = jax.random.fold_in(key, 5)
    shape = (N_ROWS, N_COLS, CAP, BLK, KS, BLK)
    first = jax.random.fold_in(key, 0)
    devices = N_ROWS * N_COLS
    index = jnp.arange(devices, dtype=jnp.float32).reshape(N_ROWS, N_COLS, 1, 1, 1, 1)
    ramp = 1.0 + 2.0 * index / max(devices - 1, 1)
    values = jax.random.truncated_normal(first, -6.0, 6.0, shape, jnp.float32)
    return jnp.clip(values * ramp, -64.0, 64.0).astype(jnp.bfloat16)


def draw_tile_coords(key, part):
    key = jax.random.fold_in(key, 11)
    first, second = jax.random.split(key)
    block_rows = jax.random.randint(first, (N_ROWS, N_COLS, CAP), 0, N_COLS, dtype=jnp.int32)
    block_cols = jax.random.randint(second, (N_ROWS, N_COLS, CAP), 0, N_ROWS * JBD, dtype=jnp.int32)
    col_ids = jnp.broadcast_to(jnp.arange(N_COLS, dtype=jnp.int32)[None, :], (N_ROWS, N_COLS))
    row_ids = jnp.broadcast_to(jnp.arange(N_ROWS, dtype=jnp.int32)[:, None] * JBD + JBD - 1, (N_ROWS, N_COLS))
    block_rows = block_rows.at[:, :, 0].set(col_ids)
    block_cols = block_cols.at[:, :, 0].set(row_ids)
    return jnp.stack([block_rows, block_cols], axis=-1)


def draw_tile_counts(key, part):
    key = jax.random.fold_in(key, 12)
    counts = jax.random.randint(key, (N_ROWS, N_COLS, 1), CAP // 2, CAP + 1, dtype=jnp.int32)
    return counts.at[:, 0, 0].set(CAP)


def steps_of(own_key, dims, pieces, low, high):
    loudness = 1.0
    for axis_at, shards_of in pieces:
        draws = jax.random.uniform(jax.random.fold_in(jax.random.fold_in(own_key, 6), axis_at), (shards_of,), jnp.float32, low / len(pieces), high / len(pieces))
        loudness = loudness * jnp.repeat(jnp.exp(draws), dims[axis_at] // shards_of).reshape((-1,) + (1,) * (len(dims) - 1 - axis_at))
    return loudness


def centred(key, dims, width, bound, cuts=(), kind=jnp.bfloat16):
    entries = jax.random.normal(key, dims, jnp.float32) * width
    if len(cuts) > 0:
        entries = steps_of(key, dims, cuts, -0.22, 0.18) * entries
    return jnp.clip(entries, min=-bound, max=bound).astype(kind)


def setup_inputs(seed: int = 0) -> dict:
    arg_keys = jax.random.split(jax.random.key(seed), 8)
    tiles = draw_tiles(jax.random.fold_in(arg_keys[7], 71), 0)
    tile_coords = draw_tile_coords(jax.random.fold_in(arg_keys[7], 71), 0)
    tile_counts = draw_tile_counts(jax.random.fold_in(arg_keys[7], 71), 0)
    factor_two = centred(arg_keys[3], (NJ, RANK), 1.0, 6.0, ((0, 512),))
    factor_three = centred(arg_keys[4], (KS, RANK), 1.0, 6.0)
    sketch_two = centred(arg_keys[5], (RANK, RANK), RANK ** -0.5, 0.375)
    sketch_three = centred(arg_keys[6], (RANK, RANK), RANK ** -0.5, 0.375)
    return dict(tiles=tiles, tile_coords=tile_coords, tile_counts=tile_counts, factor_two=factor_two, factor_three=factor_three, sketch_two=sketch_two, sketch_three=sketch_three)


def device_partials(tiles_one, coords_one, count_one, group_rows, depth_factor):
    chosen = group_rows[coords_one[:, 1]]
    product = jnp.einsum('cikj,cja->cika', tiles_one.astype(jnp.float32), chosen.astype(jnp.float32), precision=lax.Precision.HIGHEST)
    partial_value = lax.optimization_barrier(jnp.sum(product * depth_factor[None, None, :, :], axis=2))
    alive = (jnp.arange(CAP, dtype=jnp.int32) < count_one).astype(jnp.float32)
    placing = (coords_one[:, 0][:, None] == jnp.arange(N_COLS, dtype=jnp.int32)[None, :]).astype(jnp.float32) * alive[:, None]
    return jnp.einsum('cb,cia->bia', placing, partial_value, precision=lax.Precision.HIGHEST)

def reference(tiles, tile_coords, tile_counts, factor_two, factor_three, sketch_two, sketch_three):
    sketched_two = jnp.dot(factor_two.astype(jnp.float32), sketch_two.astype(jnp.float32), preferred_element_type=jnp.float32).astype(jnp.bfloat16)
    sketched_three = jnp.dot(factor_three.astype(jnp.float32), sketch_three.astype(jnp.float32), preferred_element_type=jnp.float32).astype(jnp.bfloat16)
    depth_factor = lax.optimization_barrier(sketched_three).astype(jnp.float32)
    groups = sketched_two.reshape(N_COLS, N_ROWS * JBD, BLK, RANK)

    def row_group(row_index):

        def col_device(col_index):
            return device_partials(tiles[row_index, col_index], tile_coords[row_index, col_index], tile_counts[row_index, col_index, 0], groups[col_index], depth_factor)
        return lax.optimization_barrier(jnp.sum(lax.map(col_device, jnp.arange(N_COLS, dtype=jnp.int32)), axis=0))
    sketched_rows = lax.map(row_group, jnp.arange(N_ROWS, dtype=jnp.int32)).reshape(NI, RANK)
    gram = jnp.dot(sketched_rows.T, sketched_rows, precision=lax.Precision.HIGHEST)
    lower_factor = jnp.linalg.cholesky(gram)
    solved = lax.linalg.triangular_solve(lower_factor, sketched_rows.T, left_side=True, lower=True)
    return solved.T * jnp.sqrt(jnp.float32(NI))
```

```python
import functools

import jax
import jax.numpy as jnp
from jax import lax
from jax.experimental import pallas as pl
from jax.experimental.pallas import tpu as pltpu
from jax.sharding import PartitionSpec as P

BF = jnp.bfloat16
F32 = jnp.float32
MESH = pl.DeviceIdType.MESH
VMEM = pltpu.VMEM
NX, NY, NZ, NC = 4, 8, 8, 2
MIB = 1024 * 1024

TREE = {
    "y+": [(0, 0), (0, 1), (0, 2), (0, 3), (2, 0), (2, 1), (2, 2), (1, 3)],
    "y-": [(0, 0), (0, -1), (0, -2), (2, 0), (2, -1), (2, -2), (2, -3)],
    "x+": [(0, 0), (0, 1), (1, 0), (0, -1), (0, 3), (0, 2), (0, -2), (0, -3)],
    "x-": [(0, 0), (0, 1), (0, -1), (0, 2), (0, -2), (0, 3), (0, -3), (0, 4)],
}
STEP = {"y+": (0, 1), "y-": (0, -1), "x+": (1, 0), "x-": (-1, 0)}


def place(dx, dy):
    return (dx % NX, dy % NY)


def tree_plan():
    arrival = {}
    plan = []
    for slot in range(8):
        for way in ("y+", "y-", "x+", "x-"):
            if slot < len(TREE[way]):
                edge = len(plan)
                spot = place(*TREE[way][slot])
                plan.append((edge, way, spot))
                to = place(spot[0] + STEP[way][0], spot[1] + STEP[way][1])
                arrival[to] = edge
    return [(e, w, s, arrival.get(s)) for e, w, s in plan], arrival


def gather_kernel(f2_ref, s2_ref, out_ref, send_sem, recv_sem):
    r = lax.axis_index("rows")
    c = lax.axis_index("cols")
    x, y = r // NY, r % NY

    def at(dx, dy):
        return lax.rem(x + (dx % NX), NX) * NY + lax.rem(y + (dy % NY), NY)

    barrier = pltpu.get_barrier_semaphore()
    for dx, dy in STEP.values():
        pl.semaphore_signal(barrier, inc=1, device_id=(at(dx, dy), c), device_id_type=MESH)
    half = f2_ref.shape[0] // 2
    for ch in range(2):
        own = jnp.dot(f2_ref[pl.ds(ch * half, half), :], s2_ref[...], preferred_element_type=F32)
        out_ref[r, ch] = own.astype(BF)
    pl.semaphore_wait(barrier, 4)

    plan, arrival = tree_plan()

    def copy(edge, way, spot, ch):
        src = out_ref.at[at(-spot[0], -spot[1]), ch]
        return pltpu.make_async_remote_copy(
            src_ref=src, dst_ref=src, send_sem=send_sem.at[edge, ch], recv_sem=recv_sem.at[edge, ch],
            device_id=(at(*STEP[way]), c), device_id_type=MESH)

    def wait_arrival(edge, ch):
        _, way, spot, _ = plan[edge]
        to = (spot[0] + STEP[way][0], spot[1] + STEP[way][1])
        dst = out_ref.at[at(-to[0], -to[1]), ch]
        pltpu.make_async_remote_copy(
            src_ref=dst, dst_ref=dst, send_sem=send_sem.at[edge, ch], recv_sem=recv_sem.at[edge, ch],
            device_id=(at(*STEP[way]), c), device_id_type=MESH).wait_recv()

    waited = set()
    slot_of = {}
    n = 0
    for slot in range(8):
        for way in ("y+", "y-", "x+", "x-"):
            if slot < len(TREE[way]):
                slot_of[n] = slot
                n += 1
    for slot in range(8):
        for ch in range(2):
            for edge, way, spot, brought in plan:
                if slot_of[edge] != slot:
                    continue
                if brought is not None and (brought, ch) not in waited:
                    wait_arrival(brought, ch)
                    waited.add((brought, ch))
                copy(edge, way, spot, ch).start()
    for edge, way, spot, brought in plan:
        for ch in range(2):
            if (edge, ch) not in waited:
                wait_arrival(edge, ch)
    for edge, way, spot, brought in plan:
        for ch in range(2):
            copy(edge, way, spot, ch).wait_send()


def gather(f2, s2):
    half, width = f2.shape[0] // 2, s2.shape[1]
    return pl.pallas_call(
        gather_kernel,
        out_shape=jax.ShapeDtypeStruct((NX * NY, 2, half, width), BF),
        in_specs=[pl.BlockSpec(memory_space=VMEM)] * 2,
        out_specs=pl.BlockSpec(memory_space=VMEM),
        scratch_shapes=[pltpu.SemaphoreType.DMA((31, 2)), pltpu.SemaphoreType.DMA((31, 2))],
        compiler_params=pltpu.CompilerParams(collective_id=0, has_side_effects=True, vmem_limit_bytes=16 * MIB),
        name="gather",
    )(f2, s2)


def tiles_kernel(coords, count, tiles_ref, grouped_ref, f3_ref, s3_ref, out_ref):
    size, depth = tiles_ref.shape[1], tiles_ref.shape[2]
    width = s3_ref.shape[1]
    d = jnp.dot(f3_ref[...], s3_ref[...], preferred_element_type=F32).astype(BF).astype(F32)
    out_ref[...] = jnp.zeros_like(out_ref)

    def slot(s, carry):
        q = coords[2 * s + 1]
        p = coords[2 * s]
        xs = tiles_ref[s].reshape(size * depth, tiles_ref.shape[3])
        prod = jnp.dot(xs, grouped_ref[q // 2, lax.rem(q, 2)], preferred_element_type=F32)
        term = jnp.sum(prod.reshape(size, depth, width) * d[None], axis=1)
        out_ref[p] += term
        return carry

    lax.fori_loop(0, count[0], slot, 0)


def tile_products(coords, count, tiles, grouped, f3, s3):
    size = tiles.shape[1]
    width = s3.shape[1]
    return pl.pallas_call(
        tiles_kernel,
        out_shape=jax.ShapeDtypeStruct((NZ * NC, size, width), F32),
        in_specs=[pl.BlockSpec(memory_space=pltpu.SMEM)] * 2 + [pl.BlockSpec(memory_space=VMEM)] * 4,
        out_specs=pl.BlockSpec(memory_space=VMEM),
        compiler_params=pltpu.CompilerParams(vmem_limit_bytes=32 * MIB),
        name="tile_products",
    )(coords, count, tiles, grouped, f3, s3)


def split3(a):
    a1 = a.astype(BF)
    rest = a - a1.astype(F32)
    a2 = rest.astype(BF)
    a3 = (rest - a2.astype(F32)).astype(BF)
    return a1, a2, a3


CHAINS = [(0, -1, 4), (1, 1, 4), (0, 1, 3), (1, -1, 3)]


def reduce_kernel(part_ref, rows_ref, gram_ref, pair_out, pair_in, hop_out, hop_in, mine, own, xin, xsum, yin, ysum, zin,
                  s_pair, r_pair, s_hop, r_hop, s_g, r_g, s_x, r_x, s_y, r_y, s_z, r_z, s_ya, r_ya, s_xa, r_xa, s_pa, r_pa):
    r = lax.axis_index("rows")
    c = lax.axis_index("cols")
    x, y = r // NY, r % NY
    z, core = c // NC, c % NC
    other = 1 - core

    def dev(dx=0, dy=0, dz=0, flip=False):
        row = lax.rem(x + dx, NX) * NY + lax.rem(y + dy, NY)
        return (row, lax.rem(z + dz % NZ, NZ) * NC + (other if flip else core))

    partners = [dev(flip=True)]
    partners += [dev(dx=k) for k in range(1, NX)]
    partners += [dev(dy=k) for k in range(1, NY)]
    partners += [dev(dz=k) for k in range(1, NZ)]
    barrier = pltpu.get_barrier_semaphore()
    for d in partners:
        pl.semaphore_signal(barrier, inc=1, device_id=d, device_id_type=MESH)
    pl.semaphore_wait(barrier, len(partners))

    def copy(src, dst, ssem, rsem, device):
        return pltpu.make_async_remote_copy(src_ref=src, dst_ref=dst, send_sem=ssem, recv_sem=rsem, device_id=device,
                                            device_id_type=MESH)

    order = [4, 3, 5, 2, 6, 1, 7, 0]
    pair = {}
    for d in order:
        pair_out[d] = part_ref[lax.rem(z + d, NZ) * NC + other].astype(BF)
        pair[d] = copy(pair_out.at[d], pair_in.at[d], s_pair.at[d], r_pair.at[d], dev(flip=True))
        pair[d].start()
    ready = set()

    def chip_sum(d, h):
        d = d % NZ
        if d not in ready:
            pair[d].wait_recv()
            ready.add(d)
        cols = pl.ds(h * 128, 128)
        return part_ref[lax.rem(z + d, NZ) * NC + core, :, cols] + pair_in[d, :, cols].astype(F32)

    hops = {}
    for t in range(1, 5):
        for k, (h, way, length) in enumerate(CHAINS):
            if t > length:
                continue
            value = chip_sum(way * (length - t + 1), h)
            if t > 1:
                hops[k, t - 1].wait_recv()
                value = value + hop_in[k, t - 2].astype(F32)
            hop_out[k, t - 1] = value.astype(BF)
            hops[k, t] = copy(hop_out.at[k, t - 1], hop_in.at[k, t - 1], s_hop.at[k, t - 1], r_hop.at[k, t - 1], dev(dz=way))
            hops[k, t].start()
    for h in range(2):
        total = chip_sum(0, h)
        for k, (hh, way, length) in enumerate(CHAINS):
            if hh == h:
                hops[k, length].wait_recv()
                total = total + hop_in[k, length - 1].astype(F32)
        rows_ref[:, pl.ds(h * 128, 128)] = total

    def gram_half(k):
        cols = pl.ds(pl.multiple_of(k * 128, 128), 128)
        return lax.dot_general(rows_ref[...], rows_ref[:, cols], (((0,), (0,)), ((), ())),
                               precision=lax.Precision.HIGHEST, preferred_element_type=F32)

    mine[...] = gram_half(other)
    to_pair = copy(mine, xin.at[0], s_g, r_g, dev(flip=True))
    to_pair.start()
    half = gram_half(core)
    to_pair.wait_recv()
    own[...] = half + xin[0]
    xs = []
    for k in range(1, NX):
        cp = copy(own.at[pl.ds(lax.rem(x + k, NX) * 64, 64), :], xsum.at[k], s_x.at[k], r_x.at[k], dev(dx=k))
        cp.start()
        xs.append(cp)
    acc = own[pl.ds(pl.multiple_of(x * 64, 64), 64), :]
    for k in range(1, NX):
        xs[k - 1].wait_recv()
        acc = acc + xsum[k]
    ysum[...] = acc
    ys = []
    for k in range(1, NY):
        cp = copy(ysum.at[pl.ds(lax.rem(y + k, NY) * 8, 8), :], yin.at[k], s_y.at[k], r_y.at[k], dev(dy=k))
        cp.start()
        ys.append(cp)
    acc = ysum[pl.ds(pl.multiple_of(y * 8, 8), 8), :]
    for k in range(1, NY):
        ys[k - 1].wait_recv()
        acc = acc + yin[k]
    zin[z] = acc
    zs = []
    for k in range(1, NZ):
        cp = copy(zin.at[z], zin.at[z], s_z.at[k], r_z.at[k], dev(dz=k))
        cp.start()
        zs.append(cp)
    for k in range(1, NZ):
        zs[k - 1].wait_recv()
    acc = zin[0]
    for k in range(1, NZ):
        acc = acc + zin[k]
    def piece(xx, yy):
        return gram_ref.at[core, pl.ds(xx * 64 + yy * 8, 8), :]

    gram_ref[core, pl.ds(pl.multiple_of(x * 64 + y * 8, 8), 8), :] = acc
    ya = []
    for k in range(1, NY):
        cp = copy(piece(x, y), piece(x, y), s_ya.at[k], r_ya.at[k], dev(dy=k))
        cp.start()
        ya.append(cp)
    for cp in ya:
        cp.wait_recv()

    def quarter(k):
        return gram_ref.at[core, pl.ds(lax.rem(x + k, NX) * 64, 64), :]

    xa = []
    for k in range(1, NX):
        cp = copy(quarter(0), quarter(0), s_xa.at[k], r_xa.at[k], dev(dx=k))
        cp.start()
        xa.append(cp)
    pa = [copy(quarter(0), quarter(0), s_pa.at[0], r_pa.at[0], dev(flip=True))]
    pa[0].start()
    for k in range(1, NX):
        xa[k - 1].wait_recv()
        cp = copy(quarter(NX - k), quarter(NX - k), s_pa.at[k], r_pa.at[k], dev(flip=True))
        cp.start()
        pa.append(cp)
    for cp in pa:
        cp.wait_recv()
    sends = list(pair.values()) + list(hops.values()) + [to_pair] + xs + ys + zs + ya + xa + pa
    for cp in sends:
        cp.wait_send()


def reduce_all(partials):
    size, width = partials.shape[1:]
    dma = pltpu.SemaphoreType.DMA
    return pl.pallas_call(
        reduce_kernel,
        out_shape=[jax.ShapeDtypeStruct((size, width), F32), jax.ShapeDtypeStruct((2, width, 128), F32)],
        in_specs=[pl.BlockSpec(memory_space=VMEM)],
        out_specs=[pl.BlockSpec(memory_space=VMEM)] * 2,
        scratch_shapes=[
            VMEM((NZ, size, width), BF),
            VMEM((NZ, size, width), BF),
            VMEM((4, 4, size, 128), BF),
            VMEM((4, 4, size, 128), BF),
            VMEM((width, 128), F32),
            VMEM((width, 128), F32),
            VMEM((1, width, 128), F32),
            VMEM((NX, 64, 128), F32),
            VMEM((NY, 8, 128), F32),
            VMEM((64, 128), F32),
            VMEM((NZ, 8, 128), F32),
            dma((NZ,)), dma((NZ,)),
            dma((4, 4)), dma((4, 4)),
            dma, dma,
            dma((NX,)), dma((NX,)),
            dma((NY,)), dma((NY,)),
            dma((NZ,)), dma((NZ,)),
            dma((NY,)), dma((NY,)),
            dma((NX,)), dma((NX,)),
            dma((NX,)), dma((NX,)),
        ],
        compiler_params=pltpu.CompilerParams(collective_id=1, has_side_effects=True, vmem_limit_bytes=24 * MIB),
        name="reduce",
    )(partials)


def eliminate(work, base, size):
    n = work.shape[1]
    blk = work[pl.ds(base, size), :]
    ent = {}
    for k in range(size):
        col = jnp.broadcast_to(blk[:, base + k:base + k + 1], (size, 128))
        for i in range(k, size):
            ent[i, k] = col[i:i + 1, :]
    lane = lax.broadcasted_iota(jnp.int32, (1, n), 1)
    own = (lane >= base) & (lane < base + size)
    rows = []
    for i in range(size):
        rows.append(jnp.where(own, jnp.where(lane == base + i, 1.0, 0.0), blk[i:i + 1, :]))
    reps = n // 128
    for j in range(size):
        inv = 1.0 / ent[j, j]
        mult = {i: ent[i, j] * inv for i in range(j + 1, size)}
        for k in range(j + 1, size):
            for i in range(k, size):
                ent[i, k] = ent[i, k] - mult[i] * ent[k, j]
        for i in range(j + 1, size):
            rows[i] = rows[i] - jnp.concatenate([mult[i]] * reps, axis=1) * rows[j]
        scale = lax.rsqrt(ent[j, j])
        work[pl.ds(base + j, 1), :] = rows[j] * jnp.concatenate([scale] * reps, axis=1)


def inverse_factor(work, size):
    n = work.shape[0]
    for base in range(0, n, size):
        eliminate(work, base, size)
        end = base + size
        if end == n:
            break
        p1, p2, p3 = split3(work[pl.ds(base, size), :])
        rhs = jnp.concatenate([p1, p1, p1, p2, p2, p3], axis=0)
        lhs = jnp.concatenate([p1, p2, p3, p1, p2, p1], axis=0)

        def update(a, b):
            delta = lax.dot_general(lhs[:, a:b], rhs, (((0,), (0,)), ((), ())), preferred_element_type=F32)
            lane = lax.broadcasted_iota(jnp.int32, (b - a, n), 1)
            old = jnp.where((lane >= base) & (lane < end), 0.0, work[pl.ds(a, b - a), :])
            work[pl.ds(a, b - a), :] = old - delta

        update(end, end + size)
        if end + size < n:
            update(end + size, n)
    for base in range(0, n, size):
        lane = lax.broadcasted_iota(jnp.int32, (size, n), 1)
        row = lax.broadcasted_iota(jnp.int32, (size, n), 0) + base
        work[pl.ds(base, size), :] = jnp.where(lane <= row, work[pl.ds(base, size), :], 0.0)


def solve_kernel(scale, gram_ref, rows_ref, out_ref, work):
    work[:, pl.ds(0, 128)] = gram_ref[0]
    work[:, pl.ds(128, 128)] = gram_ref[1]
    inverse_factor(work, 16)
    out = lax.dot_general(rows_ref[...], work[...], (((1,), (1,)), ((), ())), precision=lax.Precision.HIGHEST,
                          preferred_element_type=F32)
    out_ref[...] = out * scale


def solve(gram, rows, scale):
    n = gram.shape[1]
    return pl.pallas_call(
        functools.partial(solve_kernel, scale),
        out_shape=jax.ShapeDtypeStruct(rows.shape, F32),
        in_specs=[pl.BlockSpec(memory_space=VMEM)] * 2,
        out_specs=pl.BlockSpec(memory_space=VMEM),
        scratch_shapes=[VMEM((n, n), F32)],
        compiler_params=pltpu.CompilerParams(vmem_limit_bytes=16 * MIB),
        name="solve",
    )(gram, rows)


def per_device(tiles, tile_coords, tile_counts, factor_two, factor_three, sketch_two, sketch_three):
    grouped = gather(factor_two, sketch_two)
    partials = tile_products(tile_coords.reshape(-1), tile_counts.reshape(-1), tiles[0, 0], grouped, factor_three, sketch_three)
    rows, gram = reduce_all(partials)
    total_rows = rows.shape[0] * lax.axis_size("rows") * lax.axis_size("cols")
    return solve(gram, rows, float(total_rows) ** 0.5)


def solution(mesh):
    return jax.shard_map(
        per_device,
        mesh=mesh,
        in_specs=(
            P("rows", "cols", None, None, None, None),
            P("rows", "cols", None, None),
            P("rows", "cols", None),
            P(("cols", "rows"), None),
            P(),
            P(),
            P(),
        ),
        out_specs=P(("rows", "cols"), None),
        check_vma=False,
    )
```

```python
import functools

import jax
import jax.numpy as jnp
from jax import lax
from jax.experimental import pallas as pl
from jax.experimental.pallas import tpu as pltpu
from jax.sharding import PartitionSpec as P

BF = jnp.bfloat16
F32 = jnp.float32
MESH = pl.DeviceIdType.MESH
VMEM = pltpu.VMEM
NX, NY, NZ, NC = 4, 8, 8, 2
MIB = 1024 * 1024

TREE = {
    "y+": [(0, 0), (0, 1), (0, 2), (0, 3), (2, 0), (2, 1), (2, 2), (1, 3)],
    "y-": [(0, 0), (0, -1), (0, -2), (2, 0), (2, -1), (2, -2), (2, -3)],
    "x+": [(0, 0), (0, 1), (1, 0), (0, -1), (0, 3), (0, 2), (0, -2), (0, -3)],
    "x-": [(0, 0), (0, 1), (0, -1), (0, 2), (0, -2), (0, 3), (0, -3), (0, 4)],
}
STEP = {"y+": (0, 1), "y-": (0, -1), "x+": (1, 0), "x-": (-1, 0)}


def place(dx, dy):
    return (dx % NX, dy % NY)


def tree_plan():
    arrival = {}
    plan = []
    for slot in range(8):
        for way in ("y+", "y-", "x+", "x-"):
            if slot < len(TREE[way]):
                edge = len(plan)
                spot = place(*TREE[way][slot])
                plan.append((edge, way, spot))
                to = place(spot[0] + STEP[way][0], spot[1] + STEP[way][1])
                arrival[to] = edge
    return [(e, w, s, arrival.get(s)) for e, w, s in plan], arrival


PARTS = 4


def gather_rows(geo, grouped, send_sem, recv_sem, between):
    x, y, c = geo

    def at(dx, dy):
        return lax.rem(x + (dx % NX), NX) * NY + lax.rem(y + (dy % NY), NY)

    plan, _ = tree_plan()

    def copy(edge, way, spot, ch):
        piece = grouped.at[2 * at(-spot[0], -spot[1]) + ch // 2, ch % 2]
        return pltpu.make_async_remote_copy(
            src_ref=piece, dst_ref=piece, send_sem=send_sem.at[edge, ch], recv_sem=recv_sem.at[edge, ch],
            device_id=(at(*STEP[way]), c), device_id_type=MESH)

    def wait_arrival(edge, ch):
        _, way, spot, _ = plan[edge]
        copy(edge, way, (spot[0] + STEP[way][0], spot[1] + STEP[way][1]), ch).wait_recv()

    waited = set()
    started = []
    by_slot = [[e for e in plan if slot_at(e) == slot] for slot in range(8)]
    step = 0
    for slot in range(8):
        for ch in range(PARTS):
            for edge, way, spot, brought in by_slot[slot]:
                if brought is not None and (brought, ch) not in waited:
                    wait_arrival(brought, ch)
                    waited.add((brought, ch))
                started.append(copy(edge, way, spot, ch))
                started[-1].start()
            between[step]()
            step += 1
    for ch in range(PARTS):
        for edge, way, spot, brought in plan:
            if (edge, ch) not in waited:
                wait_arrival(edge, ch)
    return started


def slot_at(entry):
    return [place(*p) for p in TREE[entry[1]]].index(entry[2])


def split3(a):
    a1 = a.astype(BF)
    rest = a - a1.astype(F32)
    a2 = rest.astype(BF)
    a3 = (rest - a2.astype(F32)).astype(BF)
    return a1, a2, a3


CUTS = 2
CHAINS = [(0, -1, 4), (1, 1, 4), (0, 1, 3), (1, -1, 3)]


def rows_kernel(coords_hbm, count_hbm, tiles_hbm, f2_hbm, s2_hbm, f3_hbm, s3_hbm, rows_ref, gram_ref,
                f2_ref, s2_ref, f3_ref, s3_ref, raw, tiles_ref, grouped, flat, terms, sums_ref, coords, count, table,
                pair_out, pair_in, hop_out, hop_in, mine, own, xin, plane_in, zin,
                l_sem, t_sem, s_gather, r_gather,
                s_pair, r_pair, s_hop, r_hop, s_g, r_g, s_x, r_x, s_z, r_z, s_y, r_y, s_pa, r_pa):
    r = lax.axis_index("rows")
    c = lax.axis_index("cols")
    x, y = r // NY, r % NY
    z, core = c // NC, c % NC
    other = 1 - core
    slots, size, depth = raw.shape[0], raw.shape[1], raw.shape[2]

    def dev(dx=0, dy=0, dz=0, flip=False):
        row = lax.rem(x + dx, NX) * NY + lax.rem(y + dy, NY)
        return (row, lax.rem(z + dz % NZ, NZ) * NC + (other if flip else core))

    def copy(src, dst, ssem, rsem, device):
        return pltpu.make_async_remote_copy(src_ref=src, dst_ref=dst, send_sem=ssem, recv_sem=rsem, device_id=device,
                                            device_id_type=MESH)

    partners = [dev(flip=True), dev(dx=1), dev(dx=NX - 1), dev(dy=1), dev(dy=NY - 1), dev(dz=1), dev(dz=-1)]
    barrier = pltpu.get_barrier_semaphore()
    for d in partners:
        pl.semaphore_signal(barrier, inc=1, device_id=d, device_id_type=MESH)
    local = [pltpu.make_async_copy(src, dst, l_sem.at[i]) for i, (src, dst) in enumerate(
        [(f2_hbm, f2_ref), (s2_hbm, s2_ref), (coords_hbm, coords), (count_hbm, count),
         (f3_hbm, f3_ref), (s3_hbm, s3_ref)])]
    fetch = [pltpu.make_async_copy(tiles_hbm.at[s], raw.at[s], t_sem.at[s]) for s in range(slots)]
    for cp in local + fetch:
        cp.start()
    local[0].wait()
    local[1].wait()
    block = jnp.dot(f2_ref[...], s2_ref[...], preferred_element_type=F32).astype(BF)
    grouped[pl.ds(2 * r, 2)] = block.reshape((2,) + grouped.shape[1:])
    pl.semaphore_wait(barrier, len(partners))

    def order_slots():
        local[2].wait()
        local[3].wait()
        live = count[0, 0, 0]
        key = [jnp.where(s < live, coords[0, s], NZ * NC) for s in range(slots)]
        rank = []
        for s in range(slots):
            before = jnp.int32(0)
            for t in range(slots):
                if t < s:
                    before += jnp.where(key[t] <= key[s], 1, 0)
                elif t > s:
                    before += jnp.where(key[t] < key[s], 1, 0)
            rank.append(before)
        last = jnp.int32(-1)
        for k in range(slots):
            who, here = jnp.int32(0), jnp.int32(0)
            for s in range(slots):
                hit = rank[s] == k
                who += jnp.where(hit, s, 0)
                here += jnp.where(hit, key[s], 0)
            table[0, k] = who
            table[1, k] = jnp.where(here == last, 1, 0)
            last = here
        below = jnp.int32(0)
        for b in range(NZ * NC):
            upto = jnp.int32(0)
            for s in range(slots):
                upto += jnp.where(key[s] <= b, 1, 0)
            table[2, b] = jnp.maximum(upto - 1, 0)
            table[3, b] = jnp.where(upto > below, 1, 0)
            below = upto

    part = size // 2

    def reorder(i):
        s, h = i // 2, i % 2
        if h == 0:
            fetch[s].wait()
        rows = raw[s, pl.ds(h * part, part)].astype(F32)
        flat[h] = rows.reshape(part * depth, rows.shape[2])
        for k in range(depth):
            tiles_ref[s, pl.ds(k * size + h * part, part), :] = flat[h, pl.ds(k, part, stride=depth), :].astype(BF)

    between = [lambda: None] * (8 * PARTS)
    todo = 2 * slots
    for i in range(todo):
        at = min(2 + i, 8 * PARTS - 1)
        between[at] = (lambda f, i=i: (lambda: (f(), reorder(i))))(between[at])
    between[1] = order_slots
    gathers = gather_rows((x, y, c), grouped, s_gather, r_gather, between)

    local[4].wait()
    local[5].wait()
    weight = jnp.dot(f3_ref[...], s3_ref[...], preferred_element_type=F32).astype(BF).astype(F32)
    for s in range(slots):
        sel = grouped[coords[1, s]].reshape(size, weight.shape[1])
        term = None
        for k in range(depth):
            prod = jnp.dot(tiles_ref[s, pl.ds(k * size, size), :], sel, preferred_element_type=F32) * weight[k:k + 1, :]
            term = prod if term is None else term + prod
        terms[s] = term
    total = None
    for k in range(slots):
        total = terms[table[0, k]] if k == 0 else jnp.where(table[1, k] == 1, total, 0.0) + terms[table[0, k]]
        sums_ref[k] = total

    def partial_rows(b, cols, rows):
        return jnp.where(table[3, b] == 1, sums_ref[table[2, b], rows, cols], 0.0)

    every, whole = pl.ds(0, size), pl.ds(0, weight.shape[1])

    order = [4, 3, 5, 2, 6, 1, 7, 0]
    pair = {}
    for d in order:
        pair_out[d] = partial_rows(lax.rem(z + d, NZ) * NC + other, whole, every).astype(BF)
        pair[d] = copy(pair_out.at[d], pair_in.at[d], s_pair.at[d], r_pair.at[d], dev(flip=True))
        pair[d].start()
    ready = set()

    def chip_sum(d, h, u):
        d = d % NZ
        if d not in ready:
            pair[d].wait_recv()
            ready.add(d)
        rows, cols = pl.ds(u * cut, cut), pl.ds(h * 128, 128)
        return partial_rows(lax.rem(z + d, NZ) * NC + core, cols, rows) + pair_in[d, rows, cols].astype(F32)

    cut = size // CUTS
    hops = {}
    for t in range(1, 5):
        for u in range(CUTS):
            rows = pl.ds(u * cut, cut)
            for k, (h, way, length) in enumerate(CHAINS):
                if t > length:
                    continue
                value = chip_sum(way * (length - t + 1), h, u)
                if t > 1:
                    hops[k, t - 1, u].wait_recv()
                    value = value + hop_in[k, t - 2, rows].astype(F32)
                hop_out[k, t - 1, rows] = value.astype(BF)
                hops[k, t, u] = copy(hop_out.at[k, t - 1, rows], hop_in.at[k, t - 1, rows],
                                     s_hop.at[k, t - 1, u], r_hop.at[k, t - 1, u], dev(dz=way))
                hops[k, t, u].start()
    for u in range(CUTS):
        rows = pl.ds(u * cut, cut)
        for h in range(2):
            total = chip_sum(0, h, u)
            for k, (hh, way, length) in sorted(enumerate(CHAINS), key=lambda v: v[1][2]):
                if hh == h:
                    hops[k, length, u].wait_recv()
                    total = total + hop_in[k, length - 1, rows].astype(F32)
            rows_ref[rows, pl.ds(h * 128, 128)] = total

    def gram_half(k):
        cols = pl.ds(pl.multiple_of(k * 128, 128), 128)
        return lax.dot_general(rows_ref[...], rows_ref[:, cols], (((0,), (0,)), ((), ())),
                               precision=lax.Precision.HIGHEST, preferred_element_type=F32)

    mine[...] = gram_half(other)
    to_pair = copy(mine, xin.at[0], s_g, r_g, dev(flip=True))
    to_pair.start()
    half = gram_half(core)
    to_pair.wait_recv()
    own[...] = half + xin[0]
    far_x, far_y = (2, 1, 3, 0), (4, 3, 5, 2, 6, 1, 7, 0)
    reach = [(dx, dy) for dx in far_x for dy in far_y if (dx, dy) != (0, 0)]

    def piece(ref, dx, dy):
        row = (lax.rem(x + dx % NX, NX) * NY + lax.rem(y + dy % NY, NY)) * 8
        return ref.at[pl.ds(pl.multiple_of(row, 8), 8), :]

    spread = {}
    for dx, dy in reach:
        spread[dx, dy] = copy(piece(own, dx, dy), plane_in.at[dx, dy], s_x.at[dx, dy], r_x.at[dx, dy], dev(dx=dx, dy=dy))
        spread[dx, dy].start()
    acc = piece(own, 0, 0)[...]
    for dx, dy in reversed(reach):
        spread[dx, dy].wait_recv()
        acc = acc + plane_in[dx, dy]
    zin[z] = acc
    zs = []
    for k in (4, 3, 5, 2, 6, 1, 7):
        cp = copy(zin.at[z], zin.at[z], s_z.at[k], r_z.at[k], dev(dz=k))
        cp.start()
        zs.append(cp)
    for cp in zs:
        cp.wait_recv()
    acc = zin[0]
    for k in range(1, NZ):
        acc = acc + zin[k]
    half_ref = gram_ref.at[core]
    piece(half_ref, 0, 0)[...] = acc
    back = {}
    for dx, dy in reach:
        back[dx, dy] = copy(piece(half_ref, 0, 0), piece(half_ref, 0, 0), s_y.at[dx, dy], r_y.at[dx, dy], dev(dx=dx, dy=dy))
        back[dx, dy].start()
    pa = []
    for dx in reversed(far_x):
        for dy in reversed(far_y):
            if (dx, dy) != (0, 0):
                back[dx, dy].wait_recv()
        quarter = half_ref.at[pl.ds(pl.multiple_of(lax.rem(x + (NX - dx), NX) * 64, 64), 64), :]
        cp = copy(quarter, quarter, s_pa.at[dx], r_pa.at[dx], dev(flip=True))
        cp.start()
        pa.append(cp)
    for cp in pa:
        cp.wait_recv()
    sends = gathers + list(pair.values()) + list(hops.values()) + [to_pair] + list(spread.values()) + zs + list(back.values()) + pa
    for cp in sends:
        cp.wait_send()


def new_rows(coords, count, tiles, f2, f3, s2, s3):
    slots, size, depth, inner = tiles.shape
    width = s2.shape[1]
    dma = pltpu.SemaphoreType.DMA
    hbm = pl.BlockSpec(memory_space=pltpu.HBM)
    return pl.pallas_call(
        rows_kernel,
        out_shape=[jax.ShapeDtypeStruct((size, width), F32), jax.ShapeDtypeStruct((2, width, 128), F32)],
        in_specs=[hbm] * 7,
        out_specs=[pl.BlockSpec(memory_space=VMEM)] * 2,
        scratch_shapes=[
            VMEM(f2.shape, BF),
            VMEM(s2.shape, BF),
            VMEM(f3.shape, BF),
            VMEM(s3.shape, BF),
            VMEM(tiles.shape, BF),
            VMEM((slots, depth * size, inner), BF),
            VMEM((2 * NX * NY, 2, f2.shape[0] // PARTS, width), BF),
            VMEM((2, size * depth // 2, inner), F32),
            VMEM((slots, size, width), F32),
            VMEM((slots, size, width), F32),
            pltpu.SMEM(coords.shape, jnp.int32),
            pltpu.SMEM(count.shape, jnp.int32),
            pltpu.SMEM((4, slots), jnp.int32),
            VMEM((NZ, size, width), BF),
            VMEM((NZ, size, width), BF),
            VMEM((4, 4, size, 128), BF),
            VMEM((4, 4, size, 128), BF),
            VMEM((width, 128), F32),
            VMEM((width, 128), F32),
            VMEM((1, width, 128), F32),
            VMEM((NX, NY, 8, 128), F32),
            VMEM((NZ, 8, 128), F32),
            dma((6,)), dma((slots,)),
            dma((31, PARTS)), dma((31, PARTS)),
            dma((NZ,)), dma((NZ,)),
            dma((4, 4, CUTS)), dma((4, 4, CUTS)),
            dma, dma,
            dma((NX, NY)), dma((NX, NY)),
            dma((NZ,)), dma((NZ,)),
            dma((NX, NY)), dma((NX, NY)),
            dma((NX,)), dma((NX,)),
        ],
        compiler_params=pltpu.CompilerParams(collective_id=0, has_side_effects=True, vmem_limit_bytes=63 * MIB),
        name="new_rows",
    )(coords, count, tiles, f2, s2, f3, s3)


def eliminate(work, base, size, sub):
    n = work.shape[1]
    row = lax.broadcasted_iota(jnp.int32, (sub, 128), 0)
    lane = lax.broadcasted_iota(jnp.int32, (sub, 128), 1)
    parts, groups = size // sub, n // 128
    home, off = base // 128, base % 128
    panel = [[work[pl.ds(base + c * sub, sub), pl.ds(g * 128, 128)] for c in range(parts)] for g in range(groups)]
    block = list(panel[home])
    for c in range(parts):
        unit = jnp.where(lane == off + c * sub + row, 1.0, 0.0)
        panel[home][c] = jnp.where((lane >= off) & (lane < off + size), unit, block[c])
    diag = [None] * parts

    def spread(v, j):
        return jnp.broadcast_to(v[j:j + 1, :], (sub, 128))

    for s in range(parts):
        below = range(s, parts)
        first = off + s * sub
        cols = {c: [jnp.broadcast_to(block[c][:, first + k:first + k + 1], (sub, 128)) for k in range(sub)] for c in below}
        diag[s] = jnp.ones((sub, 128), F32)
        for j in range(sub):
            pivot = spread(cols[s][j], j)
            inv = 1.0 / pivot
            mult = {c: cols[c][j] * inv for c in below}
            mult[s] = jnp.where(row > j, mult[s], 0.0)
            diag[s] = jnp.where(row == j, pivot, diag[s])
            for k in range(j + 1, sub):
                top = spread(cols[s][k], j)
                for c in below:
                    cols[c][k] = cols[c][k] - mult[c] * top
            for g in panel + ([block] if s < parts - 1 else []):
                top = spread(g[s], j)
                for c in below:
                    g[c] = g[c] - mult[c] * top
    for c in range(parts):
        scale = lax.rsqrt(diag[c])
        for g in range(groups):
            work[pl.ds(base + c * sub, sub), pl.ds(g * 128, 128)] = panel[g][c] * scale


def inverse_factor(work, size):
    n = work.shape[0]
    for base in range(0, n, size):
        eliminate(work, base, size, 16)
        end = base + size
        if end == n:
            break
        p1, p2, p3 = split3(work[pl.ds(base, size), :])
        rhs = jnp.concatenate([p1, p1, p1, p2, p2, p3], axis=0)
        lhs = jnp.concatenate([p1, p2, p3, p1, p2, p1], axis=0)

        def update(a, b):
            delta = lax.dot_general(lhs[:, a:b], rhs, (((0,), (0,)), ((), ())), preferred_element_type=F32)
            lane = lax.broadcasted_iota(jnp.int32, (b - a, n), 1)
            old = jnp.where((lane >= base) & (lane < end), 0.0, work[pl.ds(a, b - a), :])
            work[pl.ds(a, b - a), :] = old - delta

        update(end, end + size)
        if end + size < n:
            update(end + size, n)
    for base in range(0, n, size):
        lane = lax.broadcasted_iota(jnp.int32, (size, n), 1)
        row = lax.broadcasted_iota(jnp.int32, (size, n), 0) + base
        work[pl.ds(base, size), :] = jnp.where(lane <= row, work[pl.ds(base, size), :], 0.0)


def solve_kernel(scale, gram_hbm, rows_hbm, out_ref, work, rows, sem):
    copies = [pltpu.make_async_copy(gram_hbm.at[h], work.at[:, pl.ds(h * 128, 128)], sem.at[h]) for h in range(2)]
    copies.append(pltpu.make_async_copy(rows_hbm, rows, sem.at[2]))
    for cp in copies:
        cp.start()
    copies[0].wait()
    copies[1].wait()
    inverse_factor(work, 32)
    copies[2].wait()
    out = lax.dot_general(rows[...], work[...], (((1,), (1,)), ((), ())), precision=lax.Precision.HIGHEST,
                          preferred_element_type=F32)
    out_ref[...] = out * scale


def solve(gram, rows, scale):
    n = gram.shape[1]
    return pl.pallas_call(
        functools.partial(solve_kernel, scale),
        out_shape=jax.ShapeDtypeStruct(rows.shape, F32),
        in_specs=[pl.BlockSpec(memory_space=pltpu.HBM)] * 2,
        out_specs=pl.BlockSpec(memory_space=VMEM),
        scratch_shapes=[VMEM((n, n), F32), VMEM(rows.shape, F32), pltpu.SemaphoreType.DMA((3,))],
        compiler_params=pltpu.CompilerParams(vmem_limit_bytes=63 * MIB),
        name="solve",
    )(gram, rows)


def per_device(tiles, tile_coords, tile_counts, factor_two, factor_three, sketch_two, sketch_three):
    rows, gram = new_rows(tile_coords[0, 0].T, tile_counts, tiles[0, 0], factor_two, factor_three, sketch_two, sketch_three)
    total_rows = rows.shape[0] * lax.axis_size("rows") * lax.axis_size("cols")
    return solve(gram, rows, float(total_rows) ** 0.5)


def solution(mesh):
    return jax.shard_map(
        per_device,
        mesh=mesh,
        in_specs=(
            P("rows", "cols", None, None, None, None),
            P("rows", "cols", None, None),
            P("rows", "cols", None),
            P(("cols", "rows"), None),
            P(),
            P(),
            P(),
        ),
        out_specs=P(("rows", "cols"), None),
        check_vma=False,
    )
```

```python
import functools

import jax
import jax.numpy as jnp
from jax import lax
from jax.experimental import pallas as pl
from jax.experimental.pallas import tpu as pltpu
from jax.sharding import PartitionSpec as P

BF = jnp.bfloat16
F32 = jnp.float32
MESH = pl.DeviceIdType.MESH
VMEM = pltpu.VMEM
NX, NY, NZ, NC = 4, 8, 8, 2
MIB = 1024 * 1024

PARTS = 4

TREE = {
    "y+": [(0, 0), (0, 1), (0, 2), (2, 0), (0, 3), (2, 1), (1, 3), (2, 2)],
    "y-": [(0, 0), (0, -1), (2, 0), (0, -2), (2, -1), (2, -2), (2, -3)],
    "x+": [(0, 0), (1, 0), (0, 1), (0, -1), (0, 3), (0, 2), (0, -2), (0, -3)],
    "x-": [(0, 0), (0, 1), (0, -1), (0, 2), (0, -2), (0, 3), (0, -3), (0, 4)],
}
STEP = {"y+": (0, 1), "y-": (0, -1), "x+": (1, 0), "x-": (-1, 0)}
FLIP = {"y+": "y-", "y-": "y+", "x+": "x-", "x-": "x+"}


def place(dx, dy):
    return (dx % NX, dy % NY)


def trees():
    first = {w: [place(*s) for s in spots] for w, spots in TREE.items()}
    second = {(FLIP[w] if w[0] == "y" else w): [place(a, -b) for a, b in spots] for w, spots in first.items()}
    third = {w: list(spots) for w, spots in first.items()}
    third["x-"].remove(place(0, -3))
    third["y-"].append(place(-1, -2))
    fourth = {(FLIP[w] if w[0] == "x" else w): [place(-a, b) for a, b in spots] for w, spots in third.items()}
    return [first, second, third, fourth]


def tree_plan():
    plans = []
    for tree in trees():
        arrival, plan = {}, []
        for slot in range(8):
            for way in STEP:
                if slot < len(tree[way]):
                    spot = tree[way][slot]
                    arrival[place(spot[0] + STEP[way][0], spot[1] + STEP[way][1])] = len(plan)
                    plan.append((len(plan), slot, way, spot))
        plans.append([entry + (arrival.get(entry[3]),) for entry in plan])
    return plans


def gather_rows(geo, grouped, send_sem, recv_sem, between):
    x, y, c = geo

    def at(dx, dy):
        return lax.rem(x + (dx % NX), NX) * NY + lax.rem(y + (dy % NY), NY)

    plans = [tree_plan()[ch % 4] for ch in range(PARTS)]

    def copy(ch, edge, way, spot):
        piece = grouped.at[2 * at(-spot[0], -spot[1]) + ch // (PARTS // 2), ch % (PARTS // 2)]
        return pltpu.make_async_remote_copy(
            src_ref=piece, dst_ref=piece, send_sem=send_sem.at[edge, ch], recv_sem=recv_sem.at[edge, ch],
            device_id=(at(*STEP[way]), c), device_id_type=MESH)

    def wait_arrival(ch, edge):
        _, _, way, spot, _ = plans[ch][edge]
        copy(ch, edge, way, place(spot[0] + STEP[way][0], spot[1] + STEP[way][1])).wait_recv()

    waited = set()
    started = []
    step = 0
    for now in range(8):
        for ch in range(PARTS):
            for edge, slot, way, spot, brought in plans[ch]:
                if slot != now:
                    continue
                if brought is not None and (ch, brought) not in waited:
                    wait_arrival(ch, brought)
                    waited.add((ch, brought))
                started.append(copy(ch, edge, way, spot))
                started[-1].start()
            between[step]()
            step += 1
    for ch in range(PARTS):
        for entry in plans[ch]:
            if (ch, entry[0]) not in waited:
                wait_arrival(ch, entry[0])
    return started


def split3(a):
    a1 = a.astype(BF)
    rest = a - a1.astype(F32)
    a2 = rest.astype(BF)
    a3 = (rest - a2.astype(F32)).astype(BF)
    return a1, a2, a3


CUTS = 2
CHAINS = [(0, -1, 4), (1, 1, 4), (0, 1, 3), (1, -1, 3)]


def rows_kernel(scale, coords_hbm, count_hbm, tiles_hbm, f2_hbm, s2_hbm, f3_hbm, s3_hbm, out_ref,
                rows_ref, gram_ref, work, f2_ref, s2_ref, f3_ref, s3_ref, raw, tiles_ref, grouped, flat, terms, sums_ref, coords, count, table,
                pair_out, pair_in, hop_out, hop_in, rows_in, own, plane_in, zin,
                l_sem, t_sem, s_gather, r_gather,
                s_pair, r_pair, s_hop, r_hop, s_g, r_g, s_x, r_x, s_z, r_z, s_y, r_y, s_pa, r_pa):
    r = lax.axis_index("rows")
    c = lax.axis_index("cols")
    x, y = r // NY, r % NY
    z, core = c // NC, c % NC
    other = 1 - core
    slots, size, depth = raw.shape[0], raw.shape[1], raw.shape[2]

    def dev(dx=0, dy=0, dz=0, flip=False):
        row = lax.rem(x + dx, NX) * NY + lax.rem(y + dy, NY)
        return (row, lax.rem(z + dz % NZ, NZ) * NC + (other if flip else core))

    def copy(src, dst, ssem, rsem, device):
        return pltpu.make_async_remote_copy(src_ref=src, dst_ref=dst, send_sem=ssem, recv_sem=rsem, device_id=device,
                                            device_id_type=MESH)

    partners = [dev(flip=True), dev(dx=1), dev(dx=NX - 1), dev(dy=1), dev(dy=NY - 1), dev(dz=1), dev(dz=-1)]
    barrier = pltpu.get_barrier_semaphore()
    for d in partners:
        pl.semaphore_signal(barrier, inc=1, device_id=d, device_id_type=MESH)
    local = [pltpu.make_async_copy(src, dst, l_sem.at[i]) for i, (src, dst) in enumerate(
        [(f2_hbm, f2_ref), (s2_hbm, s2_ref), (coords_hbm, coords), (count_hbm, count),
         (f3_hbm, f3_ref), (s3_hbm, s3_ref)])]
    fetch = [pltpu.make_async_copy(tiles_hbm.at[s], raw.at[s], t_sem.at[s]) for s in range(slots)]
    for cp in local + fetch:
        cp.start()
    local[0].wait()
    local[1].wait()
    block = jnp.dot(f2_ref[...], s2_ref[...], preferred_element_type=F32).astype(BF)
    grouped[pl.ds(2 * r, 2)] = block.reshape((2,) + grouped.shape[1:])
    pl.semaphore_wait(barrier, len(partners))

    def order_slots():
        local[2].wait()
        local[3].wait()
        live = count[0, 0, 0]
        key = [jnp.where(s < live, coords[0, s], NZ * NC) for s in range(slots)]
        rank = []
        for s in range(slots):
            before = jnp.int32(0)
            for t in range(slots):
                if t < s:
                    before += jnp.where(key[t] <= key[s], 1, 0)
                elif t > s:
                    before += jnp.where(key[t] < key[s], 1, 0)
            rank.append(before)
        last = jnp.int32(-1)
        for k in range(slots):
            who, here = jnp.int32(0), jnp.int32(0)
            for s in range(slots):
                hit = rank[s] == k
                who += jnp.where(hit, s, 0)
                here += jnp.where(hit, key[s], 0)
            table[0, k] = who
            table[1, k] = jnp.where(here == last, 1, 0)
            last = here
        below = jnp.int32(0)
        for b in range(NZ * NC):
            upto = jnp.int32(0)
            for s in range(slots):
                upto += jnp.where(key[s] <= b, 1, 0)
            table[2, b] = jnp.maximum(upto - 1, 0)
            table[3, b] = jnp.where(upto > below, 1, 0)
            below = upto

    part = size // 2

    def reorder(i):
        s, h = i // 2, i % 2
        if h == 0:
            fetch[s].wait()
        rows = raw[s, pl.ds(h * part, part)].astype(F32)
        flat[h] = rows.reshape(part * depth, rows.shape[2])
        for k in range(depth):
            tiles_ref[s, pl.ds(k * size + h * part, part), :] = flat[h, pl.ds(k, part, stride=depth), :].astype(BF)

    between = [lambda: None] * (8 * PARTS)
    todo = 2 * slots
    for i in range(todo):
        at = min(2 + i, 8 * PARTS - 1)
        between[at] = (lambda f, i=i: (lambda: (f(), reorder(i))))(between[at])
    between[1] = order_slots
    gathers = gather_rows((x, y, c), grouped, s_gather, r_gather, between)

    local[4].wait()
    local[5].wait()
    weight = jnp.dot(f3_ref[...], s3_ref[...], preferred_element_type=F32).astype(BF).astype(F32)
    for s in range(slots):
        sel = grouped[coords[1, s]].reshape(size, weight.shape[1])
        term = None
        for k in range(depth):
            prod = jnp.dot(tiles_ref[s, pl.ds(k * size, size), :], sel, preferred_element_type=F32) * weight[k:k + 1, :]
            term = prod if term is None else term + prod
        terms[s] = term
    total = None
    for k in range(slots):
        total = terms[table[0, k]] if k == 0 else jnp.where(table[1, k] == 1, total, 0.0) + terms[table[0, k]]
        sums_ref[k] = total

    def partial_rows(b, cols, rows):
        return jnp.where(table[3, b] == 1, sums_ref[table[2, b], rows, cols], 0.0)

    every, whole = pl.ds(0, size), pl.ds(0, weight.shape[1])

    order = [4, 3, 5, 2, 6, 1, 7, 0]
    pair = {}
    for d in order:
        pair_out[d] = partial_rows(lax.rem(z + d, NZ) * NC + other, whole, every).astype(BF)
        pair[d] = copy(pair_out.at[d], pair_in.at[d], s_pair.at[d], r_pair.at[d], dev(flip=True))
        pair[d].start()
    ready = set()

    def chip_sum(d, h, u):
        d = d % NZ
        if d not in ready:
            pair[d].wait_recv()
            ready.add(d)
        rows, cols = pl.ds(u * cut, cut), pl.ds(h * 128, 128)
        return partial_rows(lax.rem(z + d, NZ) * NC + core, cols, rows) + pair_in[d, rows, cols].astype(F32)

    cut = size // CUTS
    hops = {}
    for t in range(1, 5):
        for u in range(CUTS):
            rows = pl.ds(u * cut, cut)
            for k, (h, way, length) in enumerate(CHAINS):
                if t > length:
                    continue
                value = chip_sum(way * (length - t + 1), h, u)
                if t > 1:
                    hops[k, t - 1, u].wait_recv()
                    value = value + hop_in[k, t - 2, rows].astype(F32)
                hop_out[k, t - 1, rows] = value.astype(BF)
                hops[k, t, u] = copy(hop_out.at[k, t - 1, rows], hop_in.at[k, t - 1, rows],
                                     s_hop.at[k, t - 1, u], r_hop.at[k, t - 1, u], dev(dz=way))
                hops[k, t, u].start()
    swap = []
    for u in range(CUTS):
        rows = pl.ds(u * cut, cut)
        for h in range(2):
            total = chip_sum(0, h, u)
            for k, (hh, way, length) in sorted(enumerate(CHAINS), key=lambda v: v[1][2]):
                if hh == h:
                    hops[k, length, u].wait_recv()
                    total = total + hop_in[k, length - 1, rows].astype(F32)
            rows_ref[rows, pl.ds(h * 128, 128)] = total
        swap.append(copy(rows_ref.at[rows], rows_in.at[rows], s_g.at[u], r_g.at[u], dev(flip=True)))
        swap[-1].start()

    def gram_half(ref):
        cols = pl.ds(pl.multiple_of(core * 128, 128), 128)
        return lax.dot_general(ref[...], ref[:, cols], (((0,), (0,)), ((), ())),
                               precision=lax.Precision.HIGHEST, preferred_element_type=F32)

    half = gram_half(rows_ref)
    for cp in swap:
        cp.wait_recv()
    own[...] = half + gram_half(rows_in)
    far_x, far_y = (2, 1, 3, 0), (4, 3, 5, 2, 6, 1, 7, 0)
    reach = [(dx, dy) for dx in far_x for dy in far_y if (dx, dy) != (0, 0)]

    def piece(ref, dx, dy):
        row = (lax.rem(x + dx % NX, NX) * NY + lax.rem(y + dy % NY, NY)) * 8
        return ref.at[pl.ds(pl.multiple_of(row, 8), 8), :]

    spread = {}
    for dx, dy in reach:
        spread[dx, dy] = copy(piece(own, dx, dy), plane_in.at[dx, dy], s_x.at[dx, dy], r_x.at[dx, dy], dev(dx=dx, dy=dy))
        spread[dx, dy].start()
    acc = piece(own, 0, 0)[...]
    for dx, dy in reversed(reach):
        spread[dx, dy].wait_recv()
        acc = acc + plane_in[dx, dy]
    zin[z] = acc
    zs = []
    for k in (4, 3, 5, 2, 6, 1, 7):
        cp = copy(zin.at[z], zin.at[z], s_z.at[k], r_z.at[k], dev(dz=k))
        cp.start()
        zs.append(cp)
    for cp in zs:
        cp.wait_recv()
    acc = zin[0]
    for k in range(1, NZ):
        acc = acc + zin[k]
    half_ref = gram_ref.at[core]
    piece(half_ref, 0, 0)[...] = acc
    back = {}
    for dx, dy in reach:
        back[dx, dy] = copy(piece(half_ref, 0, 0), piece(half_ref, 0, 0), s_y.at[dx, dy], r_y.at[dx, dy], dev(dx=dx, dy=dy))
        back[dx, dy].start()
    pa = []
    for dx in reversed(far_x):
        for dy in reversed(far_y):
            if (dx, dy) != (0, 0):
                back[dx, dy].wait_recv()
        quarter = half_ref.at[pl.ds(pl.multiple_of(lax.rem(x + (NX - dx), NX) * 64, 64), 64), :]
        cp = copy(quarter, quarter, s_pa.at[dx], r_pa.at[dx], dev(flip=True))
        cp.start()
        pa.append(cp)
    for cp in pa:
        cp.wait_recv()
    for h in range(2):
        work[:, pl.ds(h * 128, 128)] = gram_ref[h]
    inverse_factor(work, 32)
    out = lax.dot_general(rows_ref[...], work[...], (((1,), (1,)), ((), ())), precision=lax.Precision.HIGHEST,
                          preferred_element_type=F32)
    out_ref[...] = out * scale
    sends = gathers + list(pair.values()) + list(hops.values()) + swap + list(spread.values()) + zs + list(back.values()) + pa
    for cp in sends:
        cp.wait_send()


def new_factor(scale, coords, count, tiles, f2, f3, s2, s3):
    slots, size, depth, inner = tiles.shape
    width = s2.shape[1]
    dma = pltpu.SemaphoreType.DMA
    hbm = pl.BlockSpec(memory_space=pltpu.HBM)
    return pl.pallas_call(
        functools.partial(rows_kernel, scale),
        out_shape=jax.ShapeDtypeStruct((size, width), F32),
        in_specs=[hbm] * 7,
        out_specs=pl.BlockSpec(memory_space=VMEM),
        scratch_shapes=[
            VMEM((size, width), F32),
            VMEM((2, width, 128), F32),
            VMEM((width, width), F32),
            VMEM(f2.shape, BF),
            VMEM(s2.shape, BF),
            VMEM(f3.shape, BF),
            VMEM(s3.shape, BF),
            VMEM(tiles.shape, BF),
            VMEM((slots, depth * size, inner), BF),
            VMEM((2 * NX * NY, PARTS // 2, f2.shape[0] // PARTS, width), BF),
            VMEM((2, size * depth // 2, inner), F32),
            VMEM((slots, size, width), F32),
            VMEM((slots, size, width), F32),
            pltpu.SMEM(coords.shape, jnp.int32),
            pltpu.SMEM(count.shape, jnp.int32),
            pltpu.SMEM((4, slots), jnp.int32),
            VMEM((NZ, size, width), BF),
            VMEM((NZ, size, width), BF),
            VMEM((4, 4, size, 128), BF),
            VMEM((4, 4, size, 128), BF),
            VMEM((size, width), F32),
            VMEM((width, 128), F32),
            VMEM((NX, NY, 8, 128), F32),
            VMEM((NZ, 8, 128), F32),
            dma((6,)), dma((slots,)),
            dma((31, PARTS)), dma((31, PARTS)),
            dma((NZ,)), dma((NZ,)),
            dma((4, 4, CUTS)), dma((4, 4, CUTS)),
            dma((CUTS,)), dma((CUTS,)),
            dma((NX, NY)), dma((NX, NY)),
            dma((NZ,)), dma((NZ,)),
            dma((NX, NY)), dma((NX, NY)),
            dma((NX,)), dma((NX,)),
        ],
        compiler_params=pltpu.CompilerParams(collective_id=0, has_side_effects=True, vmem_limit_bytes=63 * MIB),
        name="new_factor",
    )(coords, count, tiles, f2, s2, f3, s3)


def eliminate(work, base, size, sub):
    n = work.shape[1]
    row = lax.broadcasted_iota(jnp.int32, (sub, 128), 0)
    lane = lax.broadcasted_iota(jnp.int32, (sub, 128), 1)
    parts, groups = size // sub, n // 128
    home, off = base // 128, base % 128
    panel = []
    for c in range(parts):
        cut = [work[pl.ds(base + c * sub, sub), pl.ds(g * 128, 128)] for g in range(groups)]
        unit = jnp.where(lane == off + c * sub + row, 1.0, 0.0)
        own = cut[home]
        cut[home] = jnp.where((lane >= off) & (lane < off + size), unit, own)
        panel.append(jnp.stack(cut + [own]))
    diag = []
    for s in range(parts):
        below = range(s, parts)
        first = off + s * sub
        cols = {c: jnp.stack([jnp.broadcast_to(panel[c][groups][:, first + k:first + k + 1], (sub, 128)) for k in range(sub)])
                for c in below}
        if s == parts - 1:
            panel = [p[:groups] for p in panel]
        pivots = jnp.ones((sub, 128), F32)
        for j in range(sub):
            pivot = jnp.broadcast_to(cols[s][0, j:j + 1], (sub, 128))
            inv = 1.0 / pivot
            mult = {c: cols[c][0] * inv for c in below}
            mult[s] = jnp.where(row > j, mult[s], 0.0)
            pivots = jnp.where(row == j, pivot, pivots)
            if j < sub - 1:
                top = cols[s][1:, j:j + 1]
                cols = {c: cols[c][1:] - mult[c][None] * top for c in below}
            top = panel[s][:, j:j + 1]
            for c in below:
                panel[c] = panel[c] - mult[c][None] * top
        diag.append(pivots)
    for c in range(parts):
        scaled = panel[c] * lax.rsqrt(diag[c])[None]
        for g in range(groups):
            work[pl.ds(base + c * sub, sub), pl.ds(g * 128, 128)] = scaled[g]


def inverse_factor(work, size):
    n = work.shape[0]
    for base in range(0, n, size):
        eliminate(work, base, size, 16)
        end = base + size
        if end == n:
            break
        p1, p2, p3 = split3(work[pl.ds(base, size), :])
        rhs = jnp.concatenate([p1, p1, p1, p2, p2, p3], axis=0)
        lhs = jnp.concatenate([p1, p2, p3, p1, p2, p1], axis=0)

        def update(a, b):
            delta = lax.dot_general(lhs[:, a:b], rhs, (((0,), (0,)), ((), ())), preferred_element_type=F32)
            lane = lax.broadcasted_iota(jnp.int32, (b - a, n), 1)
            old = jnp.where((lane >= base) & (lane < end), 0.0, work[pl.ds(a, b - a), :])
            work[pl.ds(a, b - a), :] = old - delta

        update(end, end + size)
        if end + size < n:
            update(end + size, n)
    for base in range(0, n, size):
        lane = lax.broadcasted_iota(jnp.int32, (size, n), 1)
        row = lax.broadcasted_iota(jnp.int32, (size, n), 0) + base
        work[pl.ds(base, size), :] = jnp.where(lane <= row, work[pl.ds(base, size), :], 0.0)


def per_device(tiles, tile_coords, tile_counts, factor_two, factor_three, sketch_two, sketch_three):
    total_rows = tiles.shape[3] * lax.axis_size("rows") * lax.axis_size("cols")
    return new_factor(float(total_rows) ** 0.5, tile_coords[0, 0].T, tile_counts, tiles[0, 0], factor_two, factor_three,
                      sketch_two, sketch_three)


def solution(mesh):
    return jax.shard_map(
        per_device,
        mesh=mesh,
        in_specs=(
            P("rows", "cols", None, None, None, None),
            P("rows", "cols", None, None),
            P("rows", "cols", None),
            P(("cols", "rows"), None),
            P(),
            P(),
            P(),
        ),
        out_specs=P(("rows", "cols"), None),
        check_vma=False,
    )
```

```python
import functools

import jax
import jax.numpy as jnp
from jax import lax
from jax.experimental import pallas as pl
from jax.experimental.pallas import tpu as pltpu
from jax.sharding import PartitionSpec as P

BF = jnp.bfloat16
F32 = jnp.float32
MESH = pl.DeviceIdType.MESH
VMEM = pltpu.VMEM
NX, NY, NZ, NC = 4, 8, 8, 2
MIB = 1024 * 1024

PARTS = 4

TREE = {
    "y+": [(0, 0), (0, 1), (0, 2), (2, 0), (0, 3), (2, 1), (1, 3), (2, 2)],
    "y-": [(0, 0), (0, -1), (2, 0), (0, -2), (2, -1), (2, -2), (2, -3)],
    "x+": [(0, 0), (1, 0), (0, 1), (0, -1), (0, 3), (0, 2), (0, -2), (0, -3)],
    "x-": [(0, 0), (0, 1), (0, -1), (0, 2), (0, -2), (0, 3), (0, -3), (0, 4)],
}
STEP = {"y+": (0, 1), "y-": (0, -1), "x+": (1, 0), "x-": (-1, 0)}
FLIP = {"y+": "y-", "y-": "y+", "x+": "x-", "x-": "x+"}


def place(dx, dy):
    return (dx % NX, dy % NY)


def trees():
    first = {w: [place(*s) for s in spots] for w, spots in TREE.items()}
    second = {(FLIP[w] if w[0] == "y" else w): [place(a, -b) for a, b in spots] for w, spots in first.items()}
    third = {w: list(spots) for w, spots in first.items()}
    third["x-"].remove(place(0, -3))
    third["y-"].append(place(-1, -2))
    fourth = {(FLIP[w] if w[0] == "x" else w): [place(-a, b) for a, b in spots] for w, spots in third.items()}
    return [first, second, third, fourth]


def tree_plan():
    plans = []
    for tree in trees():
        arrival, plan = {}, []
        for slot in range(8):
            for way in STEP:
                if slot < len(tree[way]):
                    spot = tree[way][slot]
                    arrival[place(spot[0] + STEP[way][0], spot[1] + STEP[way][1])] = len(plan)
                    plan.append((len(plan), slot, way, spot))
        plans.append([entry + (arrival.get(entry[3]),) for entry in plan])
    return plans


def gather_rows(geo, grouped, send_sem, recv_sem, between):
    x, y, c = geo

    def at(dx, dy):
        return lax.rem(x + (dx % NX), NX) * NY + lax.rem(y + (dy % NY), NY)

    plans = [tree_plan()[ch % 4] for ch in range(PARTS)]

    def copy(ch, edge, way, spot):
        piece = grouped.at[2 * at(-spot[0], -spot[1]) + ch // (PARTS // 2), ch % (PARTS // 2)]
        return pltpu.make_async_remote_copy(
            src_ref=piece, dst_ref=piece, send_sem=send_sem.at[edge, ch], recv_sem=recv_sem.at[edge, ch],
            device_id=(at(*STEP[way]), c), device_id_type=MESH)

    def wait_arrival(ch, edge):
        _, _, way, spot, _ = plans[ch][edge]
        copy(ch, edge, way, place(spot[0] + STEP[way][0], spot[1] + STEP[way][1])).wait_recv()

    waited = set()
    started = []
    step = 0
    for now in range(8):
        for ch in range(PARTS):
            for edge, slot, way, spot, brought in plans[ch]:
                if slot != now:
                    continue
                if brought is not None and (ch, brought) not in waited:
                    wait_arrival(ch, brought)
                    waited.add((ch, brought))
                started.append(copy(ch, edge, way, spot))
                started[-1].start()
            between[step]()
            step += 1
    for ch in range(PARTS):
        for entry in plans[ch]:
            if (ch, entry[0]) not in waited:
                wait_arrival(ch, entry[0])
    return started


def split3(a):
    a1 = a.astype(BF)
    rest = a - a1.astype(F32)
    a2 = rest.astype(BF)
    a3 = (rest - a2.astype(F32)).astype(BF)
    return a1, a2, a3


CUTS = 2
CHAINS = [(0, -1, 4), (1, 1, 4), (0, 1, 3), (1, -1, 3)]


def rows_kernel(scale, coords_hbm, count_hbm, tiles_hbm, f2_hbm, s2_hbm, f3_hbm, s3_hbm, out_ref,
                rows_ref, gram_ref, work, f2_ref, s2_ref, f3_ref, s3_ref, raw, tiles_ref, grouped, flat, sums_ref, coords, count, table,
                pair_out, pair_in, hop_out, hop_in, rows_in, own, plane_in, zin,
                l_sem, t_sem, s_gather, r_gather,
                s_pair, r_pair, s_hop, r_hop, s_g, r_g, s_x, r_x, s_z, r_z, s_y, r_y, s_pa, r_pa):
    r = lax.axis_index("rows")
    c = lax.axis_index("cols")
    x, y = r // NY, r % NY
    z, core = c // NC, c % NC
    other = 1 - core
    slots, size, depth = raw.shape[0], raw.shape[1], raw.shape[2]

    def dev(dx=0, dy=0, dz=0, flip=False):
        row = lax.rem(x + dx, NX) * NY + lax.rem(y + dy, NY)
        return (row, lax.rem(z + dz % NZ, NZ) * NC + (other if flip else core))

    def copy(src, dst, ssem, rsem, device):
        return pltpu.make_async_remote_copy(src_ref=src, dst_ref=dst, send_sem=ssem, recv_sem=rsem, device_id=device,
                                            device_id_type=MESH)

    partners = [dev(flip=True), dev(dx=1), dev(dx=NX - 1), dev(dy=1), dev(dy=NY - 1), dev(dz=1), dev(dz=-1)]
    barrier = pltpu.get_barrier_semaphore()
    for d in partners:
        pl.semaphore_signal(barrier, inc=1, device_id=d, device_id_type=MESH)
    local = [pltpu.make_async_copy(src, dst, l_sem.at[i]) for i, (src, dst) in enumerate(
        [(f2_hbm, f2_ref), (s2_hbm, s2_ref), (coords_hbm, coords), (count_hbm, count),
         (f3_hbm, f3_ref), (s3_hbm, s3_ref)])]
    fetch = [pltpu.make_async_copy(tiles_hbm.at[s], raw.at[s], t_sem.at[s]) for s in range(slots)]
    for cp in local + fetch:
        cp.start()
    local[0].wait()
    local[1].wait()
    block = jnp.dot(f2_ref[...], s2_ref[...], preferred_element_type=F32).astype(BF)
    grouped[pl.ds(2 * r, 2)] = block.reshape((2,) + grouped.shape[1:])
    pl.semaphore_wait(barrier, len(partners))

    def order_slots():
        local[2].wait()
        local[3].wait()
        live = count[0, 0, 0]
        key = [jnp.where(s < live, coords[0, s], NZ * NC) for s in range(slots)]
        rank = []
        for s in range(slots):
            before = jnp.int32(0)
            for t in range(slots):
                if t < s:
                    before += jnp.where(key[t] <= key[s], 1, 0)
                elif t > s:
                    before += jnp.where(key[t] < key[s], 1, 0)
            rank.append(before)
        last = jnp.int32(-1)
        for k in range(slots):
            who, here = jnp.int32(0), jnp.int32(0)
            for s in range(slots):
                hit = rank[s] == k
                who += jnp.where(hit, s, 0)
                here += jnp.where(hit, key[s], 0)
            table[0, k] = who
            table[1, k] = jnp.where(here == last, 1, 0)
            last = here
        below = jnp.int32(0)
        for b in range(NZ * NC):
            upto = jnp.int32(0)
            for s in range(slots):
                upto += jnp.where(key[s] <= b, 1, 0)
            table[2, b] = jnp.maximum(upto - 1, 0)
            table[3, b] = jnp.where(upto > below, 1, 0)
            below = upto

    part = size // 2

    def reorder(i):
        s, h = i // 2, i % 2
        if h == 0:
            fetch[s].wait()
        rows = raw[s, pl.ds(h * part, part)].astype(F32)
        flat[h] = rows.reshape(part * depth, rows.shape[2])
        for k in range(depth):
            tiles_ref[s, pl.ds(k * size + h * part, part), :] = flat[h, pl.ds(k, part, stride=depth), :].astype(BF)

    between = [lambda: None] * (8 * PARTS)
    todo = 2 * slots
    for i in range(todo):
        at = min(2 + i, 8 * PARTS - 1)
        between[at] = (lambda f, i=i: (lambda: (f(), reorder(i))))(between[at])
    weights = []

    def depth_weights():
        local[4].wait()
        local[5].wait()
        weights.append(jnp.dot(f3_ref[...], s3_ref[...], preferred_element_type=F32).astype(BF).astype(F32))

    between[0] = depth_weights
    between[1] = order_slots
    gathers = gather_rows((x, y, c), grouped, s_gather, r_gather, between)

    weight = weights[0]
    total = None
    for k in range(slots):
        s = table[0, k]
        sel = grouped[coords[1, s]].reshape(size, weight.shape[1])
        term = None
        for d in range(depth):
            prod = jnp.dot(tiles_ref[s, pl.ds(d * size, size), :], sel, preferred_element_type=F32) * weight[d:d + 1, :]
            term = prod if term is None else term + prod
        total = term if k == 0 else jnp.where(table[1, k] == 1, total, 0.0) + term
        sums_ref[k] = total

    def partial_rows(b, cols, rows):
        return jnp.where(table[3, b] == 1, sums_ref[table[2, b], rows, cols], 0.0)

    every, whole = pl.ds(0, size), pl.ds(0, weight.shape[1])

    order = [4, 3, 5, 2, 6, 1, 7, 0]
    pair = {}
    for d in order:
        pair_out[d] = partial_rows(lax.rem(z + d, NZ) * NC + other, whole, every).astype(BF)
        pair[d] = copy(pair_out.at[d], pair_in.at[d], s_pair.at[d], r_pair.at[d], dev(flip=True))
        pair[d].start()
    ready = set()

    def chip_sum(d, h, u):
        d = d % NZ
        if d not in ready:
            pair[d].wait_recv()
            ready.add(d)
        rows, cols = pl.ds(u * cut, cut), pl.ds(h * 128, 128)
        return partial_rows(lax.rem(z + d, NZ) * NC + core, cols, rows) + pair_in[d, rows, cols].astype(F32)

    cut = size // CUTS
    hops = {}
    for t in range(1, 5):
        for u in range(CUTS):
            rows = pl.ds(u * cut, cut)
            for k, (h, way, length) in enumerate(CHAINS):
                if t > length:
                    continue
                value = chip_sum(way * (length - t + 1), h, u)
                if t > 1:
                    hops[k, t - 1, u].wait_recv()
                    value = value + hop_in[k, t - 2, rows].astype(F32)
                hop_out[k, t - 1, rows] = value.astype(BF)
                hops[k, t, u] = copy(hop_out.at[k, t - 1, rows], hop_in.at[k, t - 1, rows],
                                     s_hop.at[k, t - 1, u], r_hop.at[k, t - 1, u], dev(dz=way))
                hops[k, t, u].start()
    swap = []
    for u in range(CUTS):
        rows = pl.ds(u * cut, cut)
        for h in range(2):
            total = chip_sum(0, h, u)
            for k, (hh, way, length) in sorted(enumerate(CHAINS), key=lambda v: v[1][2]):
                if hh == h:
                    hops[k, length, u].wait_recv()
                    total = total + hop_in[k, length - 1, rows].astype(F32)
            rows_ref[rows, pl.ds(h * 128, 128)] = total
        swap.append(copy(rows_ref.at[rows], rows_in.at[rows], s_g.at[u], r_g.at[u], dev(flip=True)))
        swap[-1].start()

    def gram_half(ref):
        cols = pl.ds(pl.multiple_of(core * 128, 128), 128)
        return lax.dot_general(ref[...], ref[:, cols], (((0,), (0,)), ((), ())),
                               precision=lax.Precision.HIGHEST, preferred_element_type=F32)

    half = gram_half(rows_ref)
    for cp in swap:
        cp.wait_recv()
    own[...] = half + gram_half(rows_in)
    far_x, far_y = (2, 1, 3, 0), (4, 3, 5, 2, 6, 1, 7, 0)
    reach = [(dx, dy) for dx in far_x for dy in far_y if (dx, dy) != (0, 0)]

    def piece(ref, dx, dy):
        row = (lax.rem(x + dx % NX, NX) * NY + lax.rem(y + dy % NY, NY)) * 8
        return ref.at[pl.ds(pl.multiple_of(row, 8), 8), :]

    spread = {}
    for dx, dy in reach:
        spread[dx, dy] = copy(piece(own, dx, dy), plane_in.at[dx, dy], s_x.at[dx, dy], r_x.at[dx, dy], dev(dx=dx, dy=dy))
        spread[dx, dy].start()
    acc = piece(own, 0, 0)[...]
    for dx, dy in reversed(reach):
        spread[dx, dy].wait_recv()
        acc = acc + plane_in[dx, dy]
    zin[z] = acc
    zs = []
    for k in (4, 3, 5, 2, 6, 1, 7):
        cp = copy(zin.at[z], zin.at[z], s_z.at[k], r_z.at[k], dev(dz=k))
        cp.start()
        zs.append(cp)
    for cp in zs:
        cp.wait_recv()
    acc = zin[0]
    for k in range(1, NZ):
        acc = acc + zin[k]
    half_ref = gram_ref.at[core]
    piece(half_ref, 0, 0)[...] = acc
    back = {}
    for dx, dy in reach:
        back[dx, dy] = copy(piece(half_ref, 0, 0), piece(half_ref, 0, 0), s_y.at[dx, dy], r_y.at[dx, dy], dev(dx=dx, dy=dy))
        back[dx, dy].start()
    pa = []
    for dx in reversed(far_x):
        for dy in reversed(far_y):
            if (dx, dy) != (0, 0):
                back[dx, dy].wait_recv()
        quarter = half_ref.at[pl.ds(pl.multiple_of(lax.rem(x + (NX - dx), NX) * 64, 64), 64), :]
        cp = copy(quarter, quarter, s_pa.at[dx], r_pa.at[dx], dev(flip=True))
        cp.start()
        pa.append(cp)
    for cp in pa:
        cp.wait_recv()
    for h in range(2):
        work[:, pl.ds(h * 128, 128)] = gram_ref[h]
    inverse_factor(work, 32)
    out = lax.dot_general(rows_ref[...], work[...], (((1,), (1,)), ((), ())), precision=lax.Precision.HIGHEST,
                          preferred_element_type=F32)
    out_ref[...] = out * scale
    sends = gathers + list(pair.values()) + list(hops.values()) + swap + list(spread.values()) + zs + list(back.values()) + pa
    for cp in sends:
        cp.wait_send()


def new_factor(scale, coords, count, tiles, f2, f3, s2, s3):
    slots, size, depth, inner = tiles.shape
    width = s2.shape[1]
    dma = pltpu.SemaphoreType.DMA
    hbm = pl.BlockSpec(memory_space=pltpu.HBM)
    return pl.pallas_call(
        functools.partial(rows_kernel, scale),
        out_shape=jax.ShapeDtypeStruct((size, width), F32),
        in_specs=[hbm] * 7,
        out_specs=pl.BlockSpec(memory_space=VMEM),
        scratch_shapes=[
            VMEM((size, width), F32),
            VMEM((2, width, 128), F32),
            VMEM((width, width), F32),
            VMEM(f2.shape, BF),
            VMEM(s2.shape, BF),
            VMEM(f3.shape, BF),
            VMEM(s3.shape, BF),
            VMEM(tiles.shape, BF),
            VMEM((slots, depth * size, inner), BF),
            VMEM((2 * NX * NY, PARTS // 2, f2.shape[0] // PARTS, width), BF),
            VMEM((2, size * depth // 2, inner), F32),
            VMEM((slots, size, width), F32),
            pltpu.SMEM(coords.shape, jnp.int32),
            pltpu.SMEM(count.shape, jnp.int32),
            pltpu.SMEM((4, slots), jnp.int32),
            VMEM((NZ, size, width), BF),
            VMEM((NZ, size, width), BF),
            VMEM((4, 4, size, 128), BF),
            VMEM((4, 4, size, 128), BF),
            VMEM((size, width), F32),
            VMEM((width, 128), F32),
            VMEM((NX, NY, 8, 128), F32),
            VMEM((NZ, 8, 128), F32),
            dma((6,)), dma((slots,)),
            dma((31, PARTS)), dma((31, PARTS)),
            dma((NZ,)), dma((NZ,)),
            dma((4, 4, CUTS)), dma((4, 4, CUTS)),
            dma((CUTS,)), dma((CUTS,)),
            dma((NX, NY)), dma((NX, NY)),
            dma((NZ,)), dma((NZ,)),
            dma((NX, NY)), dma((NX, NY)),
            dma((NX,)), dma((NX,)),
        ],
        compiler_params=pltpu.CompilerParams(collective_id=0, has_side_effects=True, vmem_limit_bytes=63 * MIB),
        name="new_factor",
    )(coords, count, tiles, f2, s2, f3, s3)


def eliminate(work, base, size, sub):
    n = work.shape[1]
    row = lax.broadcasted_iota(jnp.int32, (sub, 128), 0)
    lane = lax.broadcasted_iota(jnp.int32, (sub, 128), 1)
    parts, groups = size // sub, n // 128
    home, off = base // 128, base % 128
    panel = []
    for c in range(parts):
        cut = [work[pl.ds(base + c * sub, sub), pl.ds(g * 128, 128)] for g in range(groups)]
        unit = jnp.where(lane == off + c * sub + row, 1.0, 0.0)
        own = cut[home]
        cut[home] = jnp.where((lane >= off) & (lane < off + size), unit, own)
        panel.append(jnp.stack(cut + [own]))
    diag = []
    for s in range(parts):
        below = range(s, parts)
        first = off + s * sub
        cols = {c: jnp.stack([jnp.broadcast_to(panel[c][groups][:, first + k:first + k + 1], (sub, 128)) for k in range(sub)])
                for c in below}
        if s == parts - 1:
            panel = [p[:groups] for p in panel]
        pivots = jnp.ones((sub, 128), F32)
        for j in range(sub):
            pivot = jnp.broadcast_to(cols[s][0, j:j + 1], (sub, 128))
            inv = 1.0 / pivot
            mult = {c: cols[c][0] * inv for c in below}
            mult[s] = jnp.where(row > j, mult[s], 0.0)
            pivots = jnp.where(row == j, pivot, pivots)
            if j < sub - 1:
                top = cols[s][1:, j:j + 1]
                cols = {c: cols[c][1:] - mult[c][None] * top for c in below}
            top = panel[s][:, j:j + 1]
            for c in below:
                panel[c] = panel[c] - mult[c][None] * top
        diag.append(pivots)
    for c in range(parts):
        scaled = panel[c] * lax.rsqrt(diag[c])[None]
        for g in range(groups):
            work[pl.ds(base + c * sub, sub), pl.ds(g * 128, 128)] = scaled[g]


def inverse_factor(work, size):
    n = work.shape[0]
    for base in range(0, n, size):
        eliminate(work, base, size, 16)
        end = base + size
        if end == n:
            break
        p1, p2, p3 = split3(work[pl.ds(base, size), :])
        rhs = jnp.concatenate([p1, p1, p1, p2, p2, p3], axis=0)
        lhs = jnp.concatenate([p1, p2, p3, p1, p2, p1], axis=0)

        def update(a, b):
            delta = lax.dot_general(lhs[:, a:b], rhs, (((0,), (0,)), ((), ())), preferred_element_type=F32)
            lane = lax.broadcasted_iota(jnp.int32, (b - a, n), 1)
            old = jnp.where((lane >= base) & (lane < end), 0.0, work[pl.ds(a, b - a), :])
            work[pl.ds(a, b - a), :] = old - delta

        update(end, end + size)
        if end + size < n:
            update(end + size, n)
    for base in range(0, n, size):
        lane = lax.broadcasted_iota(jnp.int32, (size, n), 1)
        row = lax.broadcasted_iota(jnp.int32, (size, n), 0) + base
        work[pl.ds(base, size), :] = jnp.where(lane <= row, work[pl.ds(base, size), :], 0.0)


def per_device(tiles, tile_coords, tile_counts, factor_two, factor_three, sketch_two, sketch_three):
    total_rows = tiles.shape[3] * lax.axis_size("rows") * lax.axis_size("cols")
    return new_factor(float(total_rows) ** 0.5, tile_coords[0, 0].T, tile_counts, tiles[0, 0], factor_two, factor_three,
                      sketch_two, sketch_three)


def solution(mesh):
    return jax.shard_map(
        per_device,
        mesh=mesh,
        in_specs=(
            P("rows", "cols", None, None, None, None),
            P("rows", "cols", None, None),
            P("rows", "cols", None),
            P(("cols", "rows"), None),
            P(),
            P(),
            P(),
        ),
        out_specs=P(("rows", "cols"), None),
        check_vma=False,
    )
```
